256 devices in a mesh: blk: 64 (over z, y, core), fld: 4 (over x).
Axes of the slice: x: 4, y: 4, z: 8, core: 2. Of those that a mesh axis runs over, the one named last changes fastest.
Arguments:
- first_noise: bfloat16 [256, 131072], P('fld', 'blk'), may hold values from -6 to 6
- second_noise: bfloat16 [256, 131072], P('fld', 'blk'), may hold values from -6 to 6
- first_root: bfloat16 [512, 256, 256], P('blk'), may hold values from -0.375 to 0.375
- second_root: bfloat16 [512, 256, 256], P('blk'), may hold values from -0.375 to 0.375
- cond_weight: bfloat16 [512, 16, 256, 256], P('blk'), may hold values from -0.09375 to 0.09375
- cond_ids: int32 [512, 16], P('blk'), may hold values from 0 to 511, as said below
- krig_weight: bfloat16 [256, 16, 256, 512], P('blk', None, None, 'fld'), may hold values from -0.09375 to 0.09375
- stencil: int32 [256, 16], P('blk'), may hold values from 0 to 1023, as said below
Outputs:
- first_fields: bfloat16 [256, 131072], P('fld', 'blk')
- second_fields: bfloat16 [256, 131072], P('fld', 'blk')
- field_map: float32 [256, 256, 512], P(None, 'blk', 'fld')
The draws below stay inside these ranges and needn't reach their ends.
Inputs may be any that keep to these rules, and one draw needn't show every extreme that they name: `cond_ids`: ids i with the same i // 8 form the first-level blocks of one index of blk. Among the 128 ids held by one index of blk, at most 4 name blocks of any one index, and exactly 4 name blocks of some index. `stencil`: blocks of index d of blk are ids d * 8 to (d + 1) * 8 - 1 and 512 + d * 8 to 512 + (d + 1) * 8 - 1. Among the 64 ids held by one index of blk, at most 2 name blocks of any one index, and exactly 2 name blocks of some index.
All inputs are finite; a program needn't handle non-finite values.
Results may differ from the reference program's by a relative error of at most 0.0041.
Values may be sent and summed in bfloat16 or wider, within the bound.
A program may use at most 128 MiB of HBM per device.

```python
import jax
import jax.numpy as jnp
from jax import lax

FIELDS = 256
BS = 256
COND = 16
STEN = 16
CELLS = 512
NB1_DEV = 8
NB2_DEV = 8
TILE_DEV = 4
NB1 = 512
NB2 = 512
NTILE = 256
CAP = 4
CAP2 = 2
N_BLK = 64


def spread_sources(key, readers, refs, sources, capacity):

    def one_reader(reader_key):
        key_hot, key_order, key_shuffle = jax.random.split(reader_key, 3)
        hottest = jax.random.randint(key_hot, (), 0, sources)
        slots = sources * capacity
        owner = jnp.arange(slots, dtype=jnp.int32) // capacity
        scores = jax.random.permutation(key_order, slots).astype(jnp.int32)
        scores = jnp.where(owner == hottest, -1 - jnp.arange(slots, dtype=jnp.int32) % capacity, scores)
        order = jnp.argsort(scores, stable=True)
        chosen = owner[order[:refs]]
        return chosen[jax.random.permutation(key_shuffle, refs)]
    return jax.vmap(one_reader)(jax.random.split(key, readers))


def draw_cond_ids(key, part):
    key = jax.random.fold_in(key, 11)
    key_src, key_local = jax.random.split(key)
    owners = spread_sources(key_src, N_BLK, NB2_DEV * COND, N_BLK, CAP)
    local = jax.random.randint(key_local, owners.shape, 0, NB1_DEV)
    return (owners * NB1_DEV + local).reshape(NB2, COND).astype(jnp.int32)


def draw_stencil(key, part):
    key = jax.random.fold_in(key, 23)
    key_src, key_local = jax.random.split(key)
    owners = spread_sources(key_src, N_BLK, TILE_DEV * STEN, N_BLK, CAP2)
    local = jax.random.randint(key_local, owners.shape, 0, NB1_DEV + NB2_DEV)
    ids = jnp.where(local < NB1_DEV, owners * NB1_DEV + local, NB1 + owners * NB2_DEV + local - NB1_DEV)
    return ids.reshape(NTILE, STEN).astype(jnp.int32)


def block_scale(own_key, extent, cuts, smallest, largest):
    loudness, own = 1.0, jax.random.fold_in(own_key, 6)
    for axis_at, parts in cuts:
        draws = jnp.exp(jax.random.uniform(jax.random.fold_in(own, axis_at), (parts,), jnp.float32, smallest / len(cuts), largest / len(cuts)))
        loudness = loudness * jnp.repeat(draws, extent[axis_at] // parts).reshape([-1 if axis == axis_at else 1 for axis in range(len(extent))])
    return loudness


def centred(stream_key, dims, spread, limit, pieces=(), held_as=jnp.bfloat16):
    level = block_scale(stream_key, dims, pieces, -0.22, 0.18) if pieces else 1.0
    values = jax.random.normal(stream_key, dims, jnp.float32) * spread * level
    return jnp.minimum(jnp.maximum(values, -limit), limit).astype(held_as)


def setup_inputs(seed: int = 0) -> dict:
    arg_keys = jax.random.split(jax.random.key(seed), 9)
    first_noise = centred(arg_keys[0], (FIELDS, NB1 * BS), 1.0, 6.0, ((0, 4), (1, 64)))
    second_noise = centred(arg_keys[1], (FIELDS, NB2 * BS), 1.0, 6.0, ((0, 4), (1, 64)))
    first_root = centred(arg_keys[2], (NB1, BS, BS), BS ** -0.5, 0.375, ((0, 64),))
    second_root = centred(arg_keys[3], (NB2, BS, BS), BS ** -0.5, 0.375, ((0, 64),))
    cond_weight = centred(arg_keys[4], (NB2, COND, BS, BS), (COND * BS) ** -0.5, 0.09375, ((0, 64),))
    cond_ids = draw_cond_ids(jax.random.fold_in(arg_keys[8], 71), 0)
    krig_weight = centred(arg_keys[6], (NTILE, STEN, BS, CELLS), (STEN * BS) ** -0.5, 0.09375, ((0, 64), (3, 4)))
    stencil = draw_stencil(jax.random.fold_in(arg_keys[8], 71), 0)
    return dict(first_noise=first_noise, second_noise=second_noise, first_root=first_root, second_root=second_root, cond_weight=cond_weight, cond_ids=cond_ids, krig_weight=krig_weight, stencil=stencil)


def reference(first_noise, second_noise, first_root, second_root, cond_weight, cond_ids, krig_weight, stencil):
    first_blocks = jnp.einsum('fbk,bki->fbi', first_noise.reshape(FIELDS, NB1, BS).astype(jnp.float32), first_root.astype(jnp.float32))
    first_fields = first_blocks.reshape(FIELDS, NB1 * BS).astype(jnp.bfloat16)
    first_three = first_fields.reshape(FIELDS, NB1, BS)
    noise_blocks = jnp.transpose(second_noise.reshape(FIELDS, NB2, BS), (1, 0, 2))

    def second_block(inputs):
        block_ids, weight, root, noise = inputs
        rows = jnp.take(first_three, block_ids.astype(jnp.int32), axis=1).reshape(FIELDS, COND * BS)
        total = jnp.dot(rows, weight.reshape(COND * BS, BS), preferred_element_type=jnp.float32)
        total = total + jnp.dot(noise, root, preferred_element_type=jnp.float32)
        return total.astype(jnp.bfloat16)

    second_blocks = lax.map(second_block, (cond_ids, cond_weight, second_root, noise_blocks))
    second_fields = jnp.transpose(second_blocks, (1, 0, 2)).reshape(FIELDS, NB2 * BS)
    all_three = jnp.concatenate([first_three, second_fields.reshape(FIELDS, NB2, BS)], axis=1)

    def one_tile(inputs):
        block_ids, weight = inputs
        rows = jnp.take(all_three, block_ids.astype(jnp.int32), axis=1).reshape(FIELDS, STEN * BS)
        return jnp.dot(rows, weight.reshape(STEN * BS, CELLS), preferred_element_type=jnp.float32)

    tiles = lax.map(one_tile, (stencil, krig_weight))
    field_map = jnp.transpose(tiles, (1, 0, 2))
    return first_fields, second_fields, field_map
```

```python
import functools

import jax
import jax.numpy as jnp
from jax import lax
from jax.experimental import pallas as pl
from jax.experimental.pallas import tpu as pltpu
from jax.sharding import PartitionSpec as P

MESH = pl.DeviceIdType.MESH
NZ, NY, NC, NX = 8, 4, 2, 4
NB = 8
A = 3
B = NB - A
ROWS = 64
HALF = ROWS // 2
W = 256
COND = 16
STEN = 16
TILES = 4
CELLS = 128
NB1 = 512


def f32dot(a, b):
    return jnp.dot(a, b, preferred_element_type=jnp.float32)


def gather_labels():
    labels = []
    for d in (1, -1):
        labels += [("zB", s, d) for s in (1, 2, 3, 4)]
        labels += [("yA", s, d) for s in (1, 2)]
        labels += [("yB", o, s, d) for o in range(NZ) for s in (1, 2)]
        labels += [("zA", s, d, l) for s in (1, 2, 3, 4) for l in range(A)]
    labels += [("DA", o) for o in range(NZ)] + [("DB", o) for o in range(NZ)]
    return {label: i for i, label in enumerate(labels)}


LABELS = gather_labels()


class Gather:
    def __init__(self, buf, send, recv, where):
        self.buf, self.send, self.recv = buf, send, recv
        self.z, self.y, self.c, self.x = where
        self.started = []

    def zz(self, o):
        return lax.rem(self.z + o + 2 * NZ, NZ)

    def yy(self, o):
        return lax.rem(self.y + o + 2 * NY, NY)

    def half(self, d):
        return pl.ds(0 if d == 1 else HALF, HALF)

    def place(self, label, sending):
        kind = label[0]
        back = 1 if sending else 0
        c8 = self.c * NB
        if kind == "zB":
            _, s, d = label
            row = self.zz(-(s - back) * d) * NY + self.y
            cols = pl.ds(c8 + A, B)
            return self.buf.at[row, cols, self.half(d)] if s == 4 else self.buf.at[row, cols]
        if kind == "zA":
            _, s, d, l = label
            rows = pl.ds(self.zz(-(s - back) * d) * NY, NY)
            return self.buf.at[rows, c8 + l, self.half(d)] if s == 4 else self.buf.at[rows, c8 + l]
        if kind in ("yA", "yB"):
            o, s, d = (0, label[1], label[2]) if kind == "yA" else label[1:]
            row = self.zz(o) * NY + self.yy(-(s - back) * d)
            cols = pl.ds(c8, A) if kind == "yA" else pl.ds(c8 + A, B)
            return self.buf.at[row, cols, self.half(d)] if s == 2 else self.buf.at[row, cols]
        core = self.c if sending else 1 - self.c
        cols = pl.ds(core * NB, A) if kind == "DA" else pl.ds(core * NB + A, B)
        return self.buf.at[pl.ds(self.zz(label[1]) * NY, NY), cols]

    def target(self, label):
        kind = label[0]
        if kind[0] == "z":
            z, y, c = self.zz(label[2]), self.y, self.c
        elif kind[0] == "y":
            z, y, c = self.z, self.yy(label[-1]), self.c
        else:
            z, y, c = self.z, self.y, 1 - self.c
        return ((z * NY + y) * NC + c, self.x)

    def copy(self, label, sending):
        i = LABELS[label]
        part = self.place(label, sending)
        return pltpu.make_async_remote_copy(
            part, part, self.send.at[i], self.recv.at[i],
            device_id=self.target(label), device_id_type=MESH,
        )

    def start(self, *labels):
        for label in labels:
            cp = self.copy(label, True)
            cp.start()
            self.started.append(cp)

    def wait(self, *labels):
        for label in labels:
            self.copy(label, False).wait_recv()

    def begin_b(self):
        self.start(("zB", 1, 1), ("zB", 1, -1), ("yB", 0, 1, 1), ("yB", 0, 1, -1))

    def begin_a(self):
        self.start(("yA", 1, 1), ("yA", 1, -1))

    def z_b(self, s):
        for d in (1, -1):
            self.wait(("zB", s, d))
            if s < 4:
                self.start(("zB", s + 1, d))
                o = (-s * d) % NZ
                self.start(("yB", o, 1, 1), ("yB", o, 1, -1))
        if s == 4:
            self.start(("yB", 4, 1, 1), ("yB", 4, 1, -1))

    def z_a(self, s):
        for l in range(A):
            for d in (1, -1):
                self.wait(("zA", s, d, l))
                if s < 4:
                    self.start(("zA", s + 1, d, l))
        for o in sorted({(-s) % NZ, s % NZ}):
            self.start(("DA", o))

    def y_a(self):
        for d in (1, -1):
            self.wait(("yA", 1, d))
            self.start(("yA", 2, d))

    def y_a_end(self):
        self.wait(("yA", 2, 1), ("yA", 2, -1))
        for l in range(A):
            self.start(("zA", 1, 1, l), ("zA", 1, -1, l))
        self.start(("DA", 0))

    def y_b(self, *origins):
        for o in origins:
            for d in (1, -1):
                self.wait(("yB", o % NZ, 1, d))
                self.start(("yB", o % NZ, 2, d))

    def y_b_end(self, *origins):
        for o in origins:
            self.wait(("yB", o % NZ, 2, 1), ("yB", o % NZ, 2, -1))
            self.start(("DB", o % NZ))

    def run(self):
        self.y_a()
        self.z_b(1)
        self.y_a_end()
        self.y_b(0)
        self.z_b(2)
        self.y_b_end(0)
        self.z_b(3)
        self.y_b(1, -1)
        self.z_a(1)
        self.z_b(4)
        self.y_b_end(1, -1)
        self.y_b(2, -2)
        self.z_a(2)
        self.y_b_end(2, -2)
        self.y_b(3, -3)
        self.z_a(3)
        self.y_b_end(3, -3)
        self.y_b(4)
        self.z_a(4)
        self.y_b_end(4)
        for o in range(NZ):
            self.wait(("DA", o), ("DB", o))

    def finish(self):
        for cp in self.started:
            cp.wait_send()


def kernel(
    noise1_hbm, noise2_hbm, root1_hbm, root2_hbm, cond_hbm, cond_ids, krig_hbm, stencil,
    out1, out2, out_map, krig_in,
    g1, g2, weights, noise, roots, picked, mine, theirs, field_map, away,
    local, g1_send, g1_recv, g2_send, g2_recv, x_send, x_recv,
):
    blk, x = lax.axis_index("blk"), lax.axis_index("fld")
    z, y, c = blk // (NY * NC), lax.rem(blk // NC, NY), lax.rem(blk, NC)
    own = blk // NC, c * NB
    near, far = x + 1 - 2 * lax.rem(x, 2), NX - 1 - x
    first, second = (Gather(g, s, r, (z, y, c, x)) for g, s, r in ((g1, g1_send, g1_recv), (g2, g2_send, g2_recv)))

    barrier = pltpu.get_barrier_semaphore()
    for to in [first.target((k, 1, d)) for k in ("zB", "yA") for d in (1, -1)] + [
        first.target(("DA", 0)), (blk, near), (blk, far)
    ]:
        pl.semaphore_signal(barrier, inc=1, device_id=to, device_id_type=MESH)

    loads = [
        pltpu.make_async_copy(src, dst, local.at[i])
        for i, (src, dst) in enumerate(
            [(noise1_hbm, noise.at[0]), (root1_hbm, roots.at[0]), (noise2_hbm, noise.at[1]), (root2_hbm, roots.at[1])]
            + [(cond_hbm.at[b], weights.at[b]) for b in range(NB)]
        )
    ]
    for cp in loads:
        cp.start()
    loads[0].wait()
    loads[1].wait()

    @pl.loop(0, NB)
    def _(b):
        at = pl.ds(pl.multiple_of(b * W, W), W)
        block = f32dot(noise[0, :, at], roots[0, b]).astype(jnp.bfloat16)
        g1[own[0], own[1] + b] = block
        out1[:, at] = block

    pl.semaphore_wait(barrier, 7)
    first.begin_a()
    first.begin_b()

    def weight_mate(t):
        return near if t % 2 == 0 else far

    def field_mate(t):
        return far if t % 2 == 0 else near

    def x_copy(i, src, dst, mate):
        return pltpu.make_async_remote_copy(
            src, dst, x_send.at[i], x_recv.at[i], device_id=(blk, mate), device_id_type=MESH
        )

    krig_sends = [x_copy(t, krig_hbm.at[t], krig_in.at[t], weight_mate(t)) for t in range(TILES)]
    for cp in krig_sends:
        cp.start()

    first.run()
    for cp in loads[2:]:
        cp.wait()

    def second_block(b):
        at = pl.ds(pl.multiple_of(b * W, W), W)
        for k in range(COND):
            i = cond_ids[b, k]
            picked[:, k * W : (k + 1) * W] = g1[i // (NC * NB), lax.rem(i, NC * NB)]
        total = f32dot(picked[...], weights[b]) + f32dot(noise[1, :, at], roots[1, b])
        block = total.astype(jnp.bfloat16)
        g2[own[0], own[1] + b] = block
        out2[:, at] = block

    pl.loop(0, A)(second_block)
    second.begin_a()
    pl.loop(A, NB)(second_block)
    second.begin_b()

    krig_loads = []
    for t in range(TILES):
        krig_sends[t].wait_recv()
        for h, src in enumerate((krig_hbm, krig_in)):
            cp = pltpu.make_async_copy(
                src.at[t], weights.at[t, :, pl.ds(h * CELLS, CELLS)], local.at[4 + NB + 2 * t + h]
            )
            cp.start()
            krig_loads.append(cp)
    second.run()
    for cp in krig_loads:
        cp.wait()

    field_sends = [x_copy(TILES + t, mine.at[t], theirs.at[t], field_mate(t)) for t in range(TILES)]
    for t in range(TILES):
        for s in range(STEN):
            i = stencil[t, s]
            j = jnp.minimum(i, NB1 - 1)
            k = jnp.maximum(i - NB1, 0)
            one = g1[j // (NC * NB), lax.rem(j, NC * NB)]
            two = g2[k // (NC * NB), lax.rem(k, NC * NB)]
            mine[t, :, s * W : (s + 1) * W] = jnp.where(i < NB1, one, two)
        field_sends[t].start()

    map_sends = []
    for h, (fields, whose) in enumerate(((mine, lambda t: x), (theirs, field_mate))):
        for t in range(TILES):
            if h:
                field_sends[t].wait_recv()
            total = f32dot(fields[t], weights[t])
            rows = pl.ds(pl.multiple_of(whose(t) * ROWS, ROWS), ROWS)
            field_map[t, rows, :] = total[:, :CELLS]
            away[t, h] = total[:, CELLS:]
            cp = x_copy((2 + h) * TILES + t, away.at[t, h], field_map.at[t, rows], weight_mate(t))
            cp.start()
            map_sends.append(cp)
    for h in range(2):
        for t in range(TILES):
            mate = weight_mate(t)
            sender = mate if h == 0 else (NX - 1 - mate if t % 2 == 0 else mate + 1 - 2 * lax.rem(mate, 2))
            rows = pl.ds(pl.multiple_of(sender * ROWS, ROWS), ROWS)
            x_copy((2 + h) * TILES + t, away.at[t, h], field_map.at[t, rows], mate).wait_recv()
    last = pltpu.make_async_copy(field_map, out_map, local.at[4 + NB + 2 * TILES])
    last.start()
    first.finish()
    second.finish()
    for cp in krig_sends + field_sends + map_sends:
        cp.wait_send()
    last.wait()


def on_device(
    first_noise, second_noise, first_root, second_root, cond_weight, cond_ids, krig_weight, stencil
):
    bf16, f32 = jnp.bfloat16, jnp.float32
    hbm, vmem, smem = (pl.BlockSpec(memory_space=m) for m in (pl.ANY, pltpu.VMEM, pltpu.SMEM))
    n = len(LABELS)
    dma = pltpu.SemaphoreType.DMA
    first_fields, second_fields, tiles, _ = pl.pallas_call(
        kernel,
        out_shape=(
            jax.ShapeDtypeStruct((ROWS, NB * W), bf16),
            jax.ShapeDtypeStruct((ROWS, NB * W), bf16),
            jax.ShapeDtypeStruct((TILES, NX * ROWS, CELLS), f32),
            jax.ShapeDtypeStruct((TILES, STEN * W, CELLS), bf16),
        ),
        in_specs=[hbm, hbm, hbm, hbm, hbm, smem, hbm, smem],
        out_specs=(vmem, vmem, hbm, hbm),
        scratch_shapes=[
            pltpu.VMEM((NZ * NY, NC * NB, ROWS, W), bf16),
            pltpu.VMEM((NZ * NY, NC * NB, ROWS, W), bf16),
            pltpu.VMEM((NB, COND * W, W), bf16),
            pltpu.VMEM((2, ROWS, NB * W), bf16),
            pltpu.VMEM((2, NB, W, W), bf16),
            pltpu.VMEM((ROWS, COND * W), bf16),
            pltpu.VMEM((TILES, ROWS, STEN * W), bf16),
            pltpu.VMEM((TILES, ROWS, STEN * W), bf16),
            pltpu.VMEM((TILES, NX * ROWS, CELLS), f32),
            pltpu.VMEM((TILES, 2, ROWS, CELLS), f32),
            dma((4 + NB + 2 * TILES + 1,)),
            dma((n,)), dma((n,)), dma((n,)), dma((n,)),
            dma((4 * TILES,)), dma((4 * TILES,)),
        ],
        compiler_params=pltpu.CompilerParams(
            collective_id=0, has_side_effects=True, vmem_limit_bytes=60 << 20
        ),
        cost_estimate=pl.CostEstimate(flops=2300000000, bytes_accessed=30000000, transcendentals=0),
    )(
        first_noise, second_noise, first_root, second_root,
        cond_weight.reshape(NB, COND * W, W), cond_ids,
        krig_weight.reshape(TILES, STEN * W, CELLS), stencil,
    )
    return first_fields, second_fields, jnp.transpose(tiles, (1, 0, 2))


def solution(mesh):
    placed = (
        P("fld", "blk"),
        P("fld", "blk"),
        P("blk", None, None),
        P("blk", None, None),
        P("blk", None, None, None),
        P("blk", None),
        P("blk", None, None, "fld"),
        P("blk", None),
    )
    return jax.shard_map(
        on_device,
        mesh=mesh,
        in_specs=placed,
        out_specs=(P("fld", "blk"), P("fld", "blk"), P(None, "blk", "fld")),
        check_vma=False,
    )
```

```python
import functools

import jax
import jax.numpy as jnp
from jax import lax
from jax.experimental import pallas as pl
from jax.experimental.pallas import tpu as pltpu
from jax.sharding import PartitionSpec as P

MESH = pl.DeviceIdType.MESH
NZ, NY, NC, NX = 8, 4, 2, 4
NB = 8
ROWS = 64
UNIT = 16
PARTS = ((2, 7, ((0, 4), (4, 3))), (2, 6, ((0, 3), (3, 3))))
CUTS = 2
LAG = 10
W = 256
COND = 16
STEN = 16
WHOLE = 2
HALVED = 2
TILES = WHOLE + HALVED
CELLS = 128
NB1 = 512
K = STEN * W


def f32dot(a, b):
    return jnp.dot(a, b, preferred_element_type=jnp.float32)


GROUPS = ((0, 1), (1, 2), (6, 2), (3, 3))


def gather_labels():
    labels = []
    for d in (1, -1):
        labels += [("zB", s, d) for s in (1, 2, 3, 4)]
        labels += [("yA", s, d) for s in (1, 2)]
        labels += [("yB", g, s, d) for g in range(len(GROUPS)) for s in (1, 2)]
        labels += [("zA", s, d, l) for s in (1, 2, 3, 4) for l in range(CUTS)]
    labels += [("DA", g) for g in range(len(GROUPS))]
    labels += [("DB", g, None) for g in range(len(GROUPS) - 1)]
    labels += [("DB", len(GROUPS) - 1, y) for y in range(NY)]
    return {label: i for i, label in enumerate(labels)}


LABELS = gather_labels()


class Gather:
    def __init__(self, buf, send, recv, targets, part):
        self.buf, self.send, self.recv, self.targets = buf, send, recv, targets
        self.per, self.a, self.cuts = part
        self.started = []

    def units(self, core, lo, n, half=0):
        if half:
            cut = (n + (lo % 2 == 0)) // 2
            lo, n = (lo, cut) if half == 1 else (lo + cut, n - cut)
        return pl.ds(core * (NB * self.per) + lo, n)

    def place(self, label, there):
        kind, s, d = label[0], label[-2], label[-1]
        part_a, part_b = (0, self.a), (self.a, NB * self.per - self.a)
        if kind == "zB":
            return self.buf.at[-(s - 1 + there) * d % NZ, 0, self.units(0, *part_b, d if s == 4 else 0)]
        if kind == "zA":
            s, d, l = label[1:]
            units = self.units(0, *self.cuts[l], d if s == 4 else 0)
            return self.buf.at[-(s - 1 + there) * d % NZ, :, units]
        if kind == "yA":
            return self.buf.at[0, -(s - 1 + there) * d % NY, self.units(0, *part_a, d if s == 2 else 0)]
        columns = pl.ds(*GROUPS[label[1]])
        if kind == "yB":
            return self.buf.at[columns, -(s - 1 + there) * d % NY, self.units(0, *part_b, d if s == 2 else 0)]
        if kind == "DA":
            return self.buf.at[columns, :, self.units(there, *part_a)]
        return self.buf.at[columns, slice(None) if d is None else d, self.units(there, *part_b)]

    def copy(self, label):
        i = LABELS[label]
        kind = label[0]
        way = kind[0] if kind[0] == "D" else (kind[0], label[2] if kind == "zA" else label[-1])
        return pltpu.make_async_remote_copy(
            self.place(label, 0), self.place(label, 1), self.send.at[i], self.recv.at[i],
            device_id=self.targets[way], device_id_type=MESH,
        )

    def start(self, *labels):
        for label in labels:
            cp = self.copy(label)
            cp.start()
            self.started.append(cp)

    def wait(self, *labels):
        for label in labels:
            self.copy(label).wait_recv()

    def begin(self):
        self.start(("yA", 1, 1), ("zB", 1, 1), ("yA", 1, -1), ("zB", 1, -1), ("yB", 0, 1, 1), ("yB", 0, 1, -1))

    def z_b(self, s):
        for d in (1, -1):
            self.wait(("zB", s, d))
            if s < 4:
                self.start(("zB", s + 1, d))
            if s == 2:
                g = 2 if d == 1 else 1
                self.start(("yB", g, 1, 1), ("yB", g, 1, -1))
        if s == 4:
            self.start(("yB", 3, 1, 1), ("yB", 3, 1, -1), ("DB", 3, 0))

    def z_a(self, s):
        for l in range(CUTS):
            for d in (1, -1):
                self.wait(("zA", s, d, l))
                if s < 4:
                    self.start(("zA", s + 1, d, l))
        if s == 2:
            self.start(("DA", 1), ("DA", 2))
        if s == 4:
            self.start(("DA", 3))

    def y_a(self):
        for d in (1, -1):
            self.wait(("yA", 1, d))
            self.start(("yA", 2, d))

    def y_a_end(self):
        self.wait(("yA", 2, 1), ("yA", 2, -1))
        for l in range(CUTS):
            self.start(("zA", 1, 1, l), ("zA", 1, -1, l))
        self.start(("DA", 0))

    def y_b(self, *groups):
        for g in groups:
            for d in (1, -1):
                self.wait(("yB", g, 1, d))
                self.start(("yB", g, 2, d))
                if g == 3:
                    self.start(("DB", 3, -d % NY))

    def y_b_end(self, *groups):
        for g in groups:
            self.wait(("yB", g, 2, 1), ("yB", g, 2, -1))
            self.start(("DB", g, 2 if g == 3 else None))

    def steps(self):
        return [
            lambda: self.y_a(),
            lambda: self.z_b(1),
            lambda: self.y_a_end(),
            lambda: self.y_b(0),
            lambda: self.z_b(2),
            lambda: self.z_b(3),
            lambda: self.z_a(1),
            lambda: self.y_b(1, 2),
            lambda: self.z_b(4),
            lambda: self.y_b_end(0),
            lambda: self.z_a(2),
            lambda: self.y_b_end(1, 2),
            lambda: self.z_a(3),
            lambda: self.y_b(3),
            lambda: self.z_a(4),
            lambda: self.y_b_end(3),
        ]

    def run(self, between={}):
        for i, step in enumerate(self.steps()):
            step()
            for work in between.get(i, ()):
                work()

    def arrive(self):
        for label in LABELS:
            if label[0] in ("DA", "DB"):
                self.wait(label)

    def finish(self):
        for cp in self.started:
            cp.wait_send()
        self.started = []


def kernel(
    noise1_hbm, noise2_hbm, root1_hbm, root2_hbm, cond_hbm, cond_ids, krig_hbm, stencil,
    out1, out2, out_map, krig_in,
    weights, noise, roots, fields1, fields2, whole, mine, theirs, field_map, away_whole, away_halved,
    local, krig_send, krig_recv, x_send, x_recv, map_send, map_recv, *by_part,
):
    parts = range(len(PARTS))
    g1, g2, picked, g1_send, g1_recv, g2_send, g2_recv = (
        by_part[len(PARTS) * i : len(PARTS) * (i + 1)] for i in range(7)
    )
    blk, x = lax.axis_index("blk"), lax.axis_index("fld")
    z, y, c = blk // (NY * NC), lax.rem(blk // NC, NY), lax.rem(blk, NC)
    near, far = x + 1 - 2 * lax.rem(x, 2), NX - 1 - x

    def device(dz, dy, dc):
        zz, yy, cc = lax.rem(z + dz + NZ, NZ), lax.rem(y + dy + NY, NY), lax.rem(c + dc, NC)
        return ((zz * NY + yy) * NC + cc, x)

    targets = {("z", d): device(d, 0, 0) for d in (1, -1)}
    targets |= {("y", d): device(0, d, 0) for d in (1, -1)}
    targets["D"] = device(0, 0, 1)
    first = [Gather(g1[p], g1_send[p], g1_recv[p], targets, PARTS[p]) for p in parts]
    second = [Gather(g2[p], g2_send[p], g2_recv[p], targets, PARTS[p]) for p in parts]

    def along(r):
        return (blk, lax.rem(x + r + NX, NX))

    barrier = pltpu.get_barrier_semaphore()
    for to in [*targets.values(), along(1), along(2), along(3)]:
        pl.semaphore_signal(barrier, inc=1, device_id=to, device_id_type=MESH)

    counter = iter(range(100))

    def load(src, dst):
        cp = pltpu.make_async_copy(src, dst, local.at[next(counter)])
        cp.start()
        return cp

    loads = [load(noise1_hbm, noise.at[0]), load(root1_hbm, roots.at[0])]
    for cp in loads:
        cp.wait()

    def sites(b):
        return pl.ds(pl.multiple_of(b * W, W), W)

    def rows_of(p):
        return UNIT * sum(part[0] for part in PARTS[:p]), UNIT * PARTS[p][0]

    def block_of(g, p, i):
        kz, ky = ((i >> 6) - z) & (NZ - 1), ((i >> 4) - y) & (NY - 1)
        per = PARTS[p][0]
        at = pl.ds(((((i >> 3) - c) & 1) * NB + (i & (NB - 1))) * per, per)
        return g[p][kz, ky, at].reshape(per * UNIT, W)

    def put(g, out, p, b, block):
        per = PARTS[p][0]
        lo, n = rows_of(p)
        g[p][0, 0, pl.ds(b * per, per)] = block.reshape(per, UNIT, W)
        out[lo : lo + n, sites(b)] = block

    @pl.loop(0, NB)
    def _(b):
        block = f32dot(noise[0, :, sites(b)], roots[0, b]).astype(jnp.bfloat16)
        for p in parts:
            lo, n = rows_of(p)
            put(g1, fields1, p, b, block[lo : lo + n])

    pl.semaphore_wait(barrier, 8)
    first[0].begin()

    def krig_copy(i, src, dst, to):
        return pltpu.make_async_remote_copy(
            src, dst, krig_send.at[i], krig_recv.at[i], device_id=to, device_id_type=MESH
        )

    def whole_copy(t, r):
        return krig_copy(3 * t + r - 1, krig_hbm.at[t], krig_in.at[3 * t + r - 1], along(-r))

    def passed_copy(t, d):
        half = pl.ds(0 if d == 1 else K // 2, K // 2)
        src, dst = krig_in.at[3 * t + (2 if d == 1 else 0), half], krig_in.at[3 * t + 1, half]
        return krig_copy(3 * t + 1 if d == 1 else 3 * WHOLE + HALVED + t, src, dst, along(d))

    def halved_copy(t):
        i = 3 * WHOLE + t
        return krig_copy(i, krig_hbm.at[WHOLE + t], krig_in.at[i], (blk, near if t == 0 else far))

    krig_sends = [whole_copy(t, r) for t in range(WHOLE) for r in (3, 1)] + [halved_copy(t) for t in range(HALVED)]
    for cp in krig_sends:
        cp.start()
    noise2_load, root2_load = load(noise2_hbm, noise.at[1]), load(root2_hbm, roots.at[1])
    cond_loads = [load(cond_hbm.at[b], weights.at[b]) for b in range(NB)]
    out_copies = [load(fields1, out1)]

    def pass_weights():
        for t in range(WHOLE):
            for r, d in ((3, 1), (1, -1)):
                whole_copy(t, r).wait_recv()
                cp = passed_copy(t, d)
                cp.start()
                krig_sends.append(cp)

    def second_block(p, b):
        lo, n = rows_of(p)
        for k in range(COND):
            picked[p][:, k * W : (k + 1) * W] = block_of(g1, p, cond_ids[b, k])
        total = f32dot(picked[p][...], weights[b]) + f32dot(noise[1, lo : lo + n, sites(b)], roots[1, b])
        put(g2, fields2, p, b, total.astype(jnp.bfloat16))

    def second_blocks(p, lo, hi):
        return lambda: pl.loop(lo, hi)(lambda b: second_block(p, b))

    def cells(r):
        return pl.ds(CELLS * (r % 2), CELLS)

    whole_loads, halved_loads = [[] for _ in range(WHOLE)], [[] for _ in range(HALVED)]

    def load_whole():
        for t in range(WHOLE):
            whole_loads[t].append(load(krig_hbm.at[t], weights.at[2 * t, :, cells(0)]))
            for r in (1, 3):
                whole_loads[t].append(load(krig_in.at[3 * t + r - 1], weights.at[2 * t + r // 2, :, cells(r)]))

    def load_halved():
        for t in range(HALVED):
            halved_copy(t).wait_recv()
            halved_loads[t].append(load(krig_hbm.at[WHOLE + t], weights.at[2 * WHOLE + t, :, cells(0)]))
            halved_loads[t].append(load(krig_in.at[3 * WHOLE + t], weights.at[2 * WHOLE + t, :, cells(1)]))

    def load_passed():
        for t in range(WHOLE):
            for d in (1, -1):
                passed_copy(t, d).wait_recv()
            whole_loads[t].append(load(krig_in.at[3 * t + 1], weights.at[2 * t + 1, :, cells(2)]))

    def pick(p, t, into):
        lo, n = rows_of(p)
        for s in range(STEN):
            i = stencil[t, s]
            one = block_of(g1, p, jnp.minimum(i, NB1 - 1))
            two = block_of(g2, p, jnp.maximum(i - NB1, 0))
            into[lo : lo + n, s * W : (s + 1) * W] = jnp.where(i < NB1, one, two)

    def field_copy(p, t):
        rows = pl.ds(*rows_of(p))
        i = HALVED * p + t
        return pltpu.make_async_remote_copy(
            mine.at[t, rows], theirs.at[t, rows], x_send.at[i], x_recv.at[i],
            device_id=(blk, far if t == 0 else near), device_id_type=MESH,
        )

    sends = []

    def send(cp):
        cp.start()
        sends.append(cp)

    def exchange(p, t):
        pick(p, WHOLE + t, mine.at[t])
        send(field_copy(p, t))

    todo = []
    for i, gather in enumerate(first + second):
        steps = [gather.begin] + gather.steps() + [gather.arrive]
        todo += [(LAG * i + k, step) for k, step in enumerate(steps)][1 if i == 0 else 0 :]
    todo += [(17.1, cp.wait) for cp in [noise2_load, root2_load] + cond_loads]
    for p in parts:
        at = LAG * p + 17.2
        todo += [(at + w, second_blocks(p, lo, lo + 2)) for w, lo in ((0, 0), (1, 2), (2, 4), (2.5, 6))]
    todo += [(25.5, pass_weights), (30.5, load_whole), (30.6, lambda: out_copies.append(load(fields2, out2)))]
    todo += [(33.5, first[0].finish), (34.5, first[1].finish)]
    todo += [(37.2, lambda: exchange(0, 0)), (37.3, lambda: exchange(0, 1))]
    todo += [(39.2 + t, functools.partial(pick, 0, t, whole.at[t])) for t in range(WHOLE)]
    todo += [(41.5, load_halved), (42.5, second[0].finish)]
    for _, work in sorted(todo, key=lambda entry: entry[0]):
        work()

    for t in range(HALVED):
        exchange(1, t)
    load_passed()
    second[1].finish()

    def fields_of(device):
        return pl.ds(pl.multiple_of(device * ROWS, ROWS), ROWS)

    def map_copy(i, src, t, device, to):
        return pltpu.make_async_remote_copy(
            src, field_map.at[t, fields_of(device)], map_send.at[i], map_recv.at[i], device_id=to, device_id_type=MESH
        )

    for t in range(WHOLE):
        pick(1, t, whole.at[t])
        for cp in whole_loads[t]:
            cp.wait()
        for h in range(2):
            total = f32dot(whole[t], weights[2 * t + h])
            for r in (2 * h, 2 * h + 1):
                part = total[:, (r % 2) * CELLS : (r % 2 + 1) * CELLS]
                if r == 0:
                    field_map[t, fields_of(x), :] = part
                else:
                    away_whole[t, r - 1] = part
                    send(map_copy(3 * t + r - 1, away_whole.at[t, r - 1], t, x, along(r)))
    for h in range(2):
        for t in range(HALVED):
            if h == 0:
                for cp in halved_loads[t]:
                    cp.wait()
            else:
                for p in parts:
                    field_copy(p, t).wait_recv()
            total = f32dot((theirs if h else mine)[t], weights[2 * WHOLE + t])
            whose = (far if t == 0 else near) if h else x
            field_map[WHOLE + t, fields_of(whose), :] = total[:, :CELLS]
            away_halved[t, h] = total[:, CELLS:]
            send(map_copy(3 * WHOLE + 2 * t + h, away_halved.at[t, h], WHOLE + t, whose, (blk, near if t == 0 else far)))
    for t in range(WHOLE):
        for r in range(1, NX):
            map_copy(3 * t + r - 1, away_whole.at[t, r - 1], t, lax.rem(x - r + NX, NX), along(r)).wait_recv()
        out_copies.append(load(field_map.at[t], out_map.at[t]))
    for t in range(HALVED):
        for h in range(2):
            mate = near if t == 0 else far
            device = mate if h == 0 else (NX - 1 - mate if t == 0 else mate + 1 - 2 * lax.rem(mate, 2))
            map_copy(3 * WHOLE + 2 * t + h, away_halved.at[t, h], WHOLE + t, device, (blk, mate)).wait_recv()
        out_copies.append(load(field_map.at[WHOLE + t], out_map.at[WHOLE + t]))
    for cp in krig_sends + sends:
        cp.wait_send()
    for cp in out_copies:
        cp.wait()


def hand_out(first_in, second_in, map_in, first_out, second_out, map_out):
    first_out[...] = first_in[...]
    second_out[...] = second_in[...]
    for t in range(TILES):
        map_out[:, t, :] = map_in[t]


def on_device(
    first_noise, second_noise, first_root, second_root, cond_weight, cond_ids, krig_weight, stencil
):
    bf16, f32 = jnp.bfloat16, jnp.float32
    hbm, smem = (pl.BlockSpec(memory_space=m) for m in (pl.ANY, pltpu.SMEM))
    n = len(LABELS)
    dma = pltpu.SemaphoreType.DMA
    fields = jax.ShapeDtypeStruct((ROWS, NB * W), bf16)
    by_part = [pltpu.VMEM((NZ, NY, NC * NB * p[0], UNIT, W), bf16) for p in PARTS] * 2
    by_part += [pltpu.VMEM((p[0] * UNIT, COND * W), bf16) for p in PARTS]
    by_part += [dma((n,))] * (4 * len(PARTS))
    first_fields, second_fields, tiles, _ = pl.pallas_call(
        kernel,
        out_shape=(
            fields,
            fields,
            jax.ShapeDtypeStruct((TILES, NX * ROWS, CELLS), f32),
            jax.ShapeDtypeStruct((3 * WHOLE + HALVED, K, CELLS), bf16),
        ),
        in_specs=[hbm, hbm, hbm, hbm, hbm, smem, hbm, smem],
        out_specs=(hbm, hbm, hbm, hbm),
        scratch_shapes=[
            pltpu.VMEM((NB, COND * W, W), bf16),
            pltpu.VMEM((2, ROWS, NB * W), bf16),
            pltpu.VMEM((2, NB, W, W), bf16),
            pltpu.VMEM((ROWS, NB * W), bf16),
            pltpu.VMEM((ROWS, NB * W), bf16),
            pltpu.VMEM((WHOLE, ROWS, K), bf16),
            pltpu.VMEM((HALVED, ROWS, K), bf16),
            pltpu.VMEM((HALVED, ROWS, K), bf16),
            pltpu.VMEM((TILES, NX * ROWS, CELLS), f32),
            pltpu.VMEM((WHOLE, NX - 1, ROWS, CELLS), f32),
            pltpu.VMEM((HALVED, 2, ROWS, CELLS), f32),
            dma((40,)),
            dma((4 * WHOLE + HALVED,)), dma((4 * WHOLE + HALVED,)),
            dma((HALVED * len(PARTS),)), dma((HALVED * len(PARTS),)),
            dma((3 * WHOLE + 2 * HALVED,)), dma((3 * WHOLE + 2 * HALVED,)),
            *by_part,
        ],
        compiler_params=pltpu.CompilerParams(
            collective_id=0, has_side_effects=True, vmem_limit_bytes=60 << 20
        ),
        cost_estimate=pl.CostEstimate(flops=2300000000, bytes_accessed=30000000, transcendentals=0),
    )(
        first_noise, second_noise, first_root, second_root,
        cond_weight.reshape(NB, COND * W, W), cond_ids,
        krig_weight.reshape(TILES, K, CELLS), stencil,
    )
    vmem = pl.BlockSpec(memory_space=pltpu.VMEM)
    return pl.pallas_call(
        hand_out,
        out_shape=(fields, fields, jax.ShapeDtypeStruct((NX * ROWS, TILES, CELLS), f32)),
        in_specs=[vmem, vmem, vmem],
        out_specs=(vmem, vmem, vmem),
    )(first_fields, second_fields, tiles)


def solution(mesh):
    placed = (
        P("fld", "blk"),
        P("fld", "blk"),
        P("blk", None, None),
        P("blk", None, None),
        P("blk", None, None, None),
        P("blk", None),
        P("blk", None, None, "fld"),
        P("blk", None),
    )
    return jax.shard_map(
        on_device,
        mesh=mesh,
        in_specs=placed,
        out_specs=(P("fld", "blk"), P("fld", "blk"), P(None, "blk", "fld")),
        check_vma=False,
    )
```

```python
import functools

import jax
import jax.numpy as jnp
from jax import lax
from jax.experimental import pallas as pl
from jax.experimental.pallas import tpu as pltpu
from jax.sharding import PartitionSpec as P

MESH = pl.DeviceIdType.MESH
NZ, NY, NC, NX = 8, 4, 2, 4
NB = 8
ROWS = 64
UNIT = 16
PARTS = ((2, 7, ((0, 4), (4, 3))), (2, 6, ((0, 3), (3, 3))))
CUTS = 2
W = 256
COND = 16
STEN = 16
WHOLE = 2
HALVED = 2
TILES = WHOLE + HALVED
CELLS = 128
NB1 = 512
K = STEN * W


def f32dot(a, b):
    return jnp.dot(a, b, preferred_element_type=jnp.float32)


COLUMNS = (0, 1, 7, 2, 6, 3, 5, 4)
LAST = COLUMNS[-1]


def gather_steps():
    steps = [((), (("yA", 1, 1), ("zB", 1, 1), ("yA", 1, -1), ("zB", 1, -1), ("yB", 0, 1, 1), ("yB", 0, 1, -1)))]
    for d in (1, -1):
        steps += [((("yA", 1, d),), (("yA", 2, d),))]
        steps += [((("zB", s, d),), (("zB", s + 1, d),) if s < 4 else ()) for s in (1, 2, 3, 4)]
    cuts = [(d, l) for l in range(CUTS) for d in (1, -1)]
    steps += [((("yA", 2, 1), ("yA", 2, -1)), tuple(("zA", 1, *cut) for cut in cuts) + (("DA", 0),))]

    def through(kind, column, *rest):
        ways = ((1, -1),) if column == 4 else ((-1,),) if column < 4 else ((1,),)
        return tuple((kind, min(column, NZ - column), d, *rest) for way in ways for d in way)

    for o in COLUMNS[1:]:
        end = (("DB", o, 0),) if o == LAST else ()
        steps += [(through("zB", o), (("yB", o, 1, 1), ("yB", o, 1, -1)) + end)]
    for o in COLUMNS:
        for d in (1, -1):
            end = (("DB", o, -d % NY),) if o == LAST else ()
            steps += [((("yB", o, 1, d),), (("yB", o, 2, d),) + end)]
        steps += [((("yB", o, 2, 1), ("yB", o, 2, -1)), (("DB", o, 2 if o == LAST else None),))]
    for s in (1, 2, 3, 4):
        steps += [((("zA", s, *cut),), (("zA", s + 1, *cut),) if s < 4 else ()) for cut in cuts]
    for o in COLUMNS[1:]:
        steps += [(sum((through("zA", o, l) for l in range(CUTS)), ()), (("DA", o),))]
    handed = tuple(label for _, starts in steps for label in starts if label[0] in ("DA", "DB"))
    return steps + [(handed, ())]


STEPS = gather_steps()
LABELS = {label: i for i, label in enumerate(label for _, starts in STEPS for label in starts)}
ORDER = (
    101, 106, 102, 113, 107, 112, 119, 120, 111, 103, 115, 108, 114, 126, 125, 123, 122, 121, 143, 144, 131,
    132, 145, 160, 146, 159, 128, 129, 127, 104, 117, 109, 116, 124, 133, 130, 147, 148, 137, 138, 200, 149,
    162, 150, 161, 134, 105, 135, 110, 118, 139, 201, 206, 151, 152, 219, 220, 202, 213, 207, 212, 136, 140,
    153, 164, 141, 154, 163, 211, 155, 156, 221, 225, 203, 215, 208, 214, 226, 158, 222, 157, 165, 223, 142,
    244, 243, 166, 231, 232, 0, 1, 246, 259, 245, 260, 2, 228, 229, 209, 216, 3, 204, 217, 227, 224, 4, 248,
    233, 247, 300, 230, 250, 261, 249, 262, 234, 235, 210, 205, 218, 237, 238, 252, 251, 301, 306, 307, 312,
    302, 313, 319, 320, 236, 9, 254, 263, 253, 264, 256, 240, 241, 255, 239, 308, 314, 311, 303, 315, 258,
    257, 265, 323, 322, 309, 316, 326, 325, 321, 343, 242, 344, 266, 328, 329, 345, 360, 5, 346, 359, 331, 6,
    332, 304, 317, 310, 324, 7, 334, 335, 8, 347, 348, 327, 330, 349, 362, 333, 350, 361, 10, 11, 305, 318,
    400, 12, 337, 338, 336, 352, 351, 340, 341, 13, 354, 363, 353, 364, 401, 406, 407, 412, 402, 413, 419, 18,
    420, 339, 356, 355, 342, 358, 411, 357, 365, 408, 414, 422, 423, 366, 403, 415, 14, 425, 426, 15, 444,
    443, 421, 428, 446, 459, 429, 445, 460, 16, 424, 409, 416, 404, 417, 431, 432, 17, 19, 427, 448, 447, 430,
    434, 450, 461, 449, 462, 435, 410, 405, 418, 437, 438, 452, 433, 451, 436, 454, 463, 453, 464, 440, 441,
    456, 455, 439, 457, 458, 465, 442, 466,
)


class Gather:
    def __init__(self, buf, send, recv, targets, part):
        self.buf, self.send, self.recv, self.targets = buf, send, recv, targets
        self.per, self.a, self.cuts = part
        self.started, self.here = [], set()

    def units(self, core, lo, n, half=0):
        if half:
            cut = (n + (lo % 2 == 0)) // 2
            lo, n = (lo, cut) if half == 1 else (lo + cut, n - cut)
        return pl.ds(core * (NB * self.per) + lo, n)

    def place(self, label, there):
        kind, s, d = label[0], label[-2], label[-1]
        part_a, part_b = (0, self.a), (self.a, NB * self.per - self.a)
        if kind == "zB":
            return self.buf.at[-(s - 1 + there) * d % NZ, 0, self.units(0, *part_b, d if s == 4 else 0)]
        if kind == "zA":
            s, d, l = label[1:]
            units = self.units(0, *self.cuts[l], d if s == 4 else 0)
            return self.buf.at[-(s - 1 + there) * d % NZ, :, units]
        if kind == "yA":
            return self.buf.at[0, -(s - 1 + there) * d % NY, self.units(0, *part_a, d if s == 2 else 0)]
        column = label[1]
        if kind == "yB":
            return self.buf.at[column, -(s - 1 + there) * d % NY, self.units(0, *part_b, d if s == 2 else 0)]
        if kind == "DA":
            return self.buf.at[column, :, self.units(there, *part_a)]
        return self.buf.at[column, slice(None) if d is None else d, self.units(there, *part_b)]

    def copy(self, label):
        i = LABELS[label]
        kind = label[0]
        way = kind[0] if kind[0] == "D" else (kind[0], label[2] if kind == "zA" else label[-1])
        return pltpu.make_async_remote_copy(
            self.place(label, 0), self.place(label, 1), self.send.at[i], self.recv.at[i],
            device_id=self.targets[way], device_id_type=MESH,
        )

    def step(self, k):
        for label in STEPS[k][0]:
            if label not in self.here:
                self.here.add(label)
                self.copy(label).wait_recv()
        for label in STEPS[k][1]:
            cp = self.copy(label)
            cp.start()
            self.started.append(cp)

    def finish(self):
        for cp in self.started:
            cp.wait_send()
        self.started = []


def kernel(
    noise1_hbm, noise2_hbm, root1_hbm, root2_hbm, cond_hbm, cond_ids, krig_hbm, stencil,
    out1, out2, out_map, krig_in,
    weights, noise, roots, fields1, fields2, whole, mine, theirs, field_map, away_whole, away_halved,
    local, krig_send, krig_recv, x_send, x_recv, map_send, map_recv, *by_part,
):
    parts = range(len(PARTS))
    g1, g2, picked, g1_send, g1_recv, g2_send, g2_recv = (
        by_part[len(PARTS) * i : len(PARTS) * (i + 1)] for i in range(7)
    )
    blk, x = lax.axis_index("blk"), lax.axis_index("fld")
    z, y, c = blk // (NY * NC), lax.rem(blk // NC, NY), lax.rem(blk, NC)
    near, far = x + 1 - 2 * lax.rem(x, 2), NX - 1 - x

    def device(dz, dy, dc):
        zz, yy, cc = lax.rem(z + dz + NZ, NZ), lax.rem(y + dy + NY, NY), lax.rem(c + dc, NC)
        return ((zz * NY + yy) * NC + cc, x)

    targets = {("z", d): device(d, 0, 0) for d in (1, -1)}
    targets |= {("y", d): device(0, d, 0) for d in (1, -1)}
    targets["D"] = device(0, 0, 1)
    first = [Gather(g1[p], g1_send[p], g1_recv[p], targets, PARTS[p]) for p in parts]
    second = [Gather(g2[p], g2_send[p], g2_recv[p], targets, PARTS[p]) for p in parts]

    def along(r):
        return (blk, lax.rem(x + r + NX, NX))

    barrier = pltpu.get_barrier_semaphore()
    for to in [*targets.values(), along(1), along(2), along(3)]:
        pl.semaphore_signal(barrier, inc=1, device_id=to, device_id_type=MESH)

    counter = iter(range(100))

    def load(src, dst):
        cp = pltpu.make_async_copy(src, dst, local.at[next(counter)])
        cp.start()
        return cp

    loads = [load(noise1_hbm, noise.at[0]), load(root1_hbm, roots.at[0])]
    for cp in loads:
        cp.wait()

    def sites(b):
        return pl.ds(pl.multiple_of(b * W, W), W)

    def rows_of(p):
        return UNIT * sum(part[0] for part in PARTS[:p]), UNIT * PARTS[p][0]

    def block_of(g, p, i):
        kz, ky = ((i >> 6) - z) & (NZ - 1), ((i >> 4) - y) & (NY - 1)
        per = PARTS[p][0]
        at = pl.ds(((((i >> 3) - c) & 1) * NB + (i & (NB - 1))) * per, per)
        return g[p][kz, ky, at].reshape(per * UNIT, W)

    def put(g, out, p, b, block):
        per = PARTS[p][0]
        lo, n = rows_of(p)
        g[p][0, 0, pl.ds(b * per, per)] = block.reshape(per, UNIT, W)
        out[lo : lo + n, sites(b)] = block

    @pl.loop(0, NB)
    def _(b):
        block = f32dot(noise[0, :, sites(b)], roots[0, b]).astype(jnp.bfloat16)
        for p in parts:
            lo, n = rows_of(p)
            put(g1, fields1, p, b, block[lo : lo + n])

    pl.semaphore_wait(barrier, 8)
    first[0].step(0)

    def krig_copy(i, src, dst, to):
        return pltpu.make_async_remote_copy(
            src, dst, krig_send.at[i], krig_recv.at[i], device_id=to, device_id_type=MESH
        )

    def whole_copy(t, r):
        return krig_copy(3 * t + r - 1, krig_hbm.at[t], krig_in.at[3 * t + r - 1], along(-r))

    def passed_copy(t, d):
        half = pl.ds(0 if d == 1 else K // 2, K // 2)
        src, dst = krig_in.at[3 * t + (2 if d == 1 else 0), half], krig_in.at[3 * t + 1, half]
        return krig_copy(3 * t + 1 if d == 1 else 3 * WHOLE + HALVED + t, src, dst, along(d))

    def halved_copy(t):
        i = 3 * WHOLE + t
        return krig_copy(i, krig_hbm.at[WHOLE + t], krig_in.at[i], (blk, near if t == 0 else far))

    krig_sends = [whole_copy(t, r) for t in range(WHOLE) for r in (3, 1)] + [halved_copy(t) for t in range(HALVED)]
    for cp in krig_sends:
        cp.start()
    noise2_load, root2_load = load(noise2_hbm, noise.at[1]), load(root2_hbm, roots.at[1])
    cond_loads = [load(cond_hbm.at[b], weights.at[b]) for b in range(NB)]
    out_copies = [load(fields1, out1)]

    def pass_weights():
        for t in range(WHOLE):
            for r, d in ((3, 1), (1, -1)):
                whole_copy(t, r).wait_recv()
                cp = passed_copy(t, d)
                cp.start()
                krig_sends.append(cp)

    def second_block(p, b):
        lo, n = rows_of(p)
        for k in range(COND):
            picked[p][:, k * W : (k + 1) * W] = block_of(g1, p, cond_ids[b, k])
        total = f32dot(picked[p][...], weights[b]) + f32dot(noise[1, lo : lo + n, sites(b)], roots[1, b])
        put(g2, fields2, p, b, total.astype(jnp.bfloat16))

    def second_blocks(p, lo, hi):
        return lambda: pl.loop(lo, hi)(lambda b: second_block(p, b))

    def cells(r):
        return pl.ds(CELLS * (r % 2), CELLS)

    whole_loads, halved_loads = [[] for _ in range(WHOLE)], [[] for _ in range(HALVED)]

    def load_whole():
        for t in range(WHOLE):
            whole_loads[t].append(load(krig_hbm.at[t], weights.at[2 * t, :, cells(0)]))
            for r in (1, 3):
                whole_loads[t].append(load(krig_in.at[3 * t + r - 1], weights.at[2 * t + r // 2, :, cells(r)]))

    def load_halved():
        for t in range(HALVED):
            halved_copy(t).wait_recv()
            halved_loads[t].append(load(krig_hbm.at[WHOLE + t], weights.at[2 * WHOLE + t, :, cells(0)]))
            halved_loads[t].append(load(krig_in.at[3 * WHOLE + t], weights.at[2 * WHOLE + t, :, cells(1)]))

    def load_passed():
        for t in range(WHOLE):
            for d in (1, -1):
                passed_copy(t, d).wait_recv()
            whole_loads[t].append(load(krig_in.at[3 * t + 1], weights.at[2 * t + 1, :, cells(2)]))

    def pick(p, t, into):
        lo, n = rows_of(p)
        for s in range(STEN):
            i = stencil[t, s]
            one = block_of(g1, p, jnp.minimum(i, NB1 - 1))
            two = block_of(g2, p, jnp.maximum(i - NB1, 0))
            into[lo : lo + n, s * W : (s + 1) * W] = jnp.where(i < NB1, one, two)

    def field_copy(p, t):
        rows = pl.ds(*rows_of(p))
        i = HALVED * p + t
        return pltpu.make_async_remote_copy(
            mine.at[t, rows], theirs.at[t, rows], x_send.at[i], x_recv.at[i],
            device_id=(blk, far if t == 0 else near), device_id_type=MESH,
        )

    sends = []

    def send(cp):
        cp.start()
        sends.append(cp)

    def exchange(p, t):
        pick(p, WHOLE + t, mine.at[t])
        send(field_copy(p, t))

    def wait_cond():
        for cp in [noise2_load, root2_load] + cond_loads:
            cp.wait()

    def copy_second():
        out_copies.append(load(fields2, out2))

    other = [wait_cond] + [second_blocks(p, b, b + 2) for p in parts for b in range(0, NB, 2)]
    other += [pass_weights, load_whole, copy_second, first[0].finish, first[1].finish]
    other += [functools.partial(exchange, 0, t) for t in range(HALVED)]
    other += [functools.partial(pick, 0, t, whole.at[t]) for t in range(WHOLE)]
    other += [load_halved, second[0].finish]
    for k in ORDER:
        if k < 100:
            other[k]()
        else:
            (first + second)[k // 100 - 1].step(k % 100)

    for t in range(HALVED):
        exchange(1, t)
    load_passed()
    second[1].finish()

    def fields_of(device):
        return pl.ds(pl.multiple_of(device * ROWS, ROWS), ROWS)

    def map_copy(i, src, t, device, to):
        return pltpu.make_async_remote_copy(
            src, field_map.at[t, fields_of(device)], map_send.at[i], map_recv.at[i], device_id=to, device_id_type=MESH
        )

    for t in range(WHOLE):
        pick(1, t, whole.at[t])
        for cp in whole_loads[t]:
            cp.wait()
        for h in range(2):
            total = f32dot(whole[t], weights[2 * t + h])
            for r in (2 * h, 2 * h + 1):
                part = total[:, (r % 2) * CELLS : (r % 2 + 1) * CELLS]
                if r == 0:
                    field_map[t, fields_of(x), :] = part
                else:
                    away_whole[t, r - 1] = part
                    send(map_copy(3 * t + r - 1, away_whole.at[t, r - 1], t, x, along(r)))
    for h in range(2):
        for t in range(HALVED):
            if h == 0:
                for cp in halved_loads[t]:
                    cp.wait()
            else:
                for p in parts:
                    field_copy(p, t).wait_recv()
            total = f32dot((theirs if h else mine)[t], weights[2 * WHOLE + t])
            whose = (far if t == 0 else near) if h else x
            field_map[WHOLE + t, fields_of(whose), :] = total[:, :CELLS]
            away_halved[t, h] = total[:, CELLS:]
            send(map_copy(3 * WHOLE + 2 * t + h, away_halved.at[t, h], WHOLE + t, whose, (blk, near if t == 0 else far)))
    for t in range(WHOLE):
        for r in range(1, NX):
            map_copy(3 * t + r - 1, away_whole.at[t, r - 1], t, lax.rem(x - r + NX, NX), along(r)).wait_recv()
        out_copies.append(load(field_map.at[t], out_map.at[t]))
    for t in range(HALVED):
        for h in range(2):
            mate = near if t == 0 else far
            device = mate if h == 0 else (NX - 1 - mate if t == 0 else mate + 1 - 2 * lax.rem(mate, 2))
            map_copy(3 * WHOLE + 2 * t + h, away_halved.at[t, h], WHOLE + t, device, (blk, mate)).wait_recv()
        out_copies.append(load(field_map.at[WHOLE + t], out_map.at[WHOLE + t]))
    for cp in krig_sends + sends:
        cp.wait_send()
    for cp in out_copies:
        cp.wait()


def hand_out(first_in, second_in, map_in, first_out, second_out, map_out):
    first_out[...] = first_in[...]
    second_out[...] = second_in[...]
    for t in range(TILES):
        map_out[:, t, :] = map_in[t]


def on_device(
    first_noise, second_noise, first_root, second_root, cond_weight, cond_ids, krig_weight, stencil
):
    bf16, f32 = jnp.bfloat16, jnp.float32
    hbm, smem = (pl.BlockSpec(memory_space=m) for m in (pl.ANY, pltpu.SMEM))
    n = len(LABELS)
    dma = pltpu.SemaphoreType.DMA
    fields = jax.ShapeDtypeStruct((ROWS, NB * W), bf16)
    by_part = [pltpu.VMEM((NZ, NY, NC * NB * p[0], UNIT, W), bf16) for p in PARTS] * 2
    by_part += [pltpu.VMEM((p[0] * UNIT, COND * W), bf16) for p in PARTS]
    by_part += [dma((n,))] * (4 * len(PARTS))
    first_fields, second_fields, tiles, _ = pl.pallas_call(
        kernel,
        out_shape=(
            fields,
            fields,
            jax.ShapeDtypeStruct((TILES, NX * ROWS, CELLS), f32),
            jax.ShapeDtypeStruct((3 * WHOLE + HALVED, K, CELLS), bf16),
        ),
        in_specs=[hbm, hbm, hbm, hbm, hbm, smem, hbm, smem],
        out_specs=(hbm, hbm, hbm, hbm),
        scratch_shapes=[
            pltpu.VMEM((NB, COND * W, W), bf16),
            pltpu.VMEM((2, ROWS, NB * W), bf16),
            pltpu.VMEM((2, NB, W, W), bf16),
            pltpu.VMEM((ROWS, NB * W), bf16),
            pltpu.VMEM((ROWS, NB * W), bf16),
            pltpu.VMEM((WHOLE, ROWS, K), bf16),
            pltpu.VMEM((HALVED, ROWS, K), bf16),
            pltpu.VMEM((HALVED, ROWS, K), bf16),
            pltpu.VMEM((TILES, NX * ROWS, CELLS), f32),
            pltpu.VMEM((WHOLE, NX - 1, ROWS, CELLS), f32),
            pltpu.VMEM((HALVED, 2, ROWS, CELLS), f32),
            dma((40,)),
            dma((4 * WHOLE + HALVED,)), dma((4 * WHOLE + HALVED,)),
            dma((HALVED * len(PARTS),)), dma((HALVED * len(PARTS),)),
            dma((3 * WHOLE + 2 * HALVED,)), dma((3 * WHOLE + 2 * HALVED,)),
            *by_part,
        ],
        compiler_params=pltpu.CompilerParams(
            collective_id=0, has_side_effects=True, vmem_limit_bytes=60 << 20
        ),
        cost_estimate=pl.CostEstimate(flops=2300000000, bytes_accessed=30000000, transcendentals=0),
    )(
        first_noise, second_noise, first_root, second_root,
        cond_weight.reshape(NB, COND * W, W), cond_ids,
        krig_weight.reshape(TILES, K, CELLS), stencil,
    )
    vmem = pl.BlockSpec(memory_space=pltpu.VMEM)
    return pl.pallas_call(
        hand_out,
        out_shape=(fields, fields, jax.ShapeDtypeStruct((NX * ROWS, TILES, CELLS), f32)),
        in_specs=[vmem, vmem, vmem],
        out_specs=(vmem, vmem, vmem),
    )(first_fields, second_fields, tiles)


def solution(mesh):
    placed = (
        P("fld", "blk"),
        P("fld", "blk"),
        P("blk", None, None),
        P("blk", None, None),
        P("blk", None, None, None),
        P("blk", None),
        P("blk", None, None, "fld"),
        P("blk", None),
    )
    return jax.shard_map(
        on_device,
        mesh=mesh,
        in_specs=placed,
        out_specs=(P("fld", "blk"), P("fld", "blk"), P(None, "blk", "fld")),
        check_vma=False,
    )
```

```python
import functools

import jax
import jax.numpy as jnp
from jax import lax
from jax.experimental import pallas as pl
from jax.experimental.pallas import tpu as pltpu
from jax.sharding import PartitionSpec as P

MESH = pl.DeviceIdType.MESH
NZ, NY, NC, NX = 8, 4, 2, 4
NB = 8
ROWS = 64
UNIT = 16
PARTS = ((2, 7, ((0, 4), (4, 3))), (2, 6, ((0, 3), (3, 3))))
CUTS = 2
W = 256
COND = 16
STEN = 16
WHOLE = 2
HALVED = 2
TILES = WHOLE + HALVED
CELLS = 128
NB1 = 512
K = STEN * W


def f32dot(a, b):
    return jnp.dot(a, b, preferred_element_type=jnp.float32)


COLUMNS = (0, 1, 7, 2, 6, 3, 5, 4)
LAST = COLUMNS[-1]


def gather_steps():
    steps = [((), (("yA", 1, 1), ("zB", 1, 1), ("yA", 1, -1), ("zB", 1, -1), ("yB", 0, 1, 1), ("yB", 0, 1, -1)))]
    for d in (1, -1):
        steps += [((("yA", 1, d),), (("yA", 2, d),))]
        steps += [((("zB", s, d),), (("zB", s + 1, d),) if s < 4 else ()) for s in (1, 2, 3, 4)]
    cuts = [(d, l) for l in range(CUTS) for d in (1, -1)]
    steps += [((("yA", 2, 1), ("yA", 2, -1)), tuple(("zA", 1, *cut) for cut in cuts) + (("DA", 0),))]

    def through(kind, column, *rest):
        ways = ((1, -1),) if column == 4 else ((-1,),) if column < 4 else ((1,),)
        return tuple((kind, min(column, NZ - column), d, *rest) for way in ways for d in way)

    for o in COLUMNS[1:]:
        end = (("DB", o, 0),) if o == LAST else ()
        steps += [(through("zB", o), (("yB", o, 1, 1), ("yB", o, 1, -1)) + end)]
    for o in COLUMNS:
        for d in (1, -1):
            end = (("DB", o, -d % NY),) if o == LAST else ()
            steps += [((("yB", o, 1, d),), (("yB", o, 2, d),) + end)]
        steps += [((("yB", o, 2, 1), ("yB", o, 2, -1)), (("DB", o, 2 if o == LAST else None),))]
    for s in (1, 2, 3, 4):
        steps += [((("zA", s, *cut),), (("zA", s + 1, *cut),) if s < 4 else ()) for cut in cuts]
    for o in COLUMNS[1:]:
        steps += [(sum((through("zA", o, l) for l in range(CUTS)), ()), (("DA", o),))]
    handed = tuple(label for _, starts in steps for label in starts if label[0] in ("DA", "DB"))
    return steps + [(handed, ())]


STEPS = gather_steps()
LABELS = {label: i for i, label in enumerate(label for _, starts in STEPS for label in starts)}
ORDER = (
    101, 106, 102, 113, 107, 112, 119, 120, 111, 103, 115, 108, 114, 126, 125, 123, 122, 121, 143, 144, 131,
    132, 145, 160, 146, 159, 128, 129, 127, 104, 117, 109, 116, 124, 133, 130, 147, 148, 137, 138, 200, 149,
    162, 150, 161, 134, 105, 135, 110, 118, 139, 201, 206, 151, 152, 219, 220, 202, 213, 207, 212, 136, 140,
    153, 164, 141, 154, 163, 211, 155, 156, 221, 225, 203, 215, 208, 214, 226, 158, 222, 157, 165, 223, 142,
    244, 243, 166, 231, 232, 0, 1, 246, 259, 245, 260, 2, 228, 229, 209, 216, 3, 204, 217, 227, 224, 4, 248,
    233, 247, 300, 230, 250, 261, 249, 262, 234, 235, 210, 205, 218, 237, 238, 252, 251, 301, 306, 307, 312,
    302, 313, 319, 320, 236, 9, 254, 263, 253, 264, 256, 240, 241, 255, 239, 308, 314, 311, 303, 315, 258,
    257, 265, 323, 322, 309, 316, 326, 325, 321, 343, 242, 344, 266, 328, 329, 345, 360, 5, 346, 359, 331, 6,
    332, 304, 317, 310, 324, 7, 334, 335, 8, 347, 348, 327, 330, 349, 362, 333, 350, 361, 10, 11, 305, 318,
    400, 12, 337, 338, 336, 352, 351, 340, 341, 13, 354, 363, 353, 364, 401, 406, 407, 412, 402, 413, 419, 18,
    420, 339, 356, 355, 342, 358, 411, 357, 365, 408, 414, 422, 423, 366, 403, 415, 14, 425, 426, 15, 444,
    443, 421, 428, 446, 459, 429, 445, 460, 16, 424, 409, 416, 404, 417, 431, 432, 17, 19, 427, 448, 447, 430,
    434, 450, 461, 449, 462, 435, 410, 405, 418, 437, 438, 452, 433, 451, 436, 454, 463, 453, 464, 440, 441,
    456, 455, 439, 457, 458, 465, 442, 466,
)


class Gather:
    def __init__(self, buf, send, recv, targets, part):
        self.buf, self.send, self.recv, self.targets = buf, send, recv, targets
        self.per, self.a, self.cuts = part
        self.started, self.here = [], set()

    def units(self, core, lo, n, half=0):
        if half:
            cut = (n + (lo % 2 == 0)) // 2
            lo, n = (lo, cut) if half == 1 else (lo + cut, n - cut)
        return pl.ds(core * (NB * self.per) + lo, n)

    def place(self, label, there):
        kind, s, d = label[0], label[-2], label[-1]
        part_a, part_b = (0, self.a), (self.a, NB * self.per - self.a)
        if kind == "zB":
            return self.buf.at[-(s - 1 + there) * d % NZ, 0, self.units(0, *part_b, d if s == 4 else 0)]
        if kind == "zA":
            s, d, l = label[1:]
            units = self.units(0, *self.cuts[l], d if s == 4 else 0)
            return self.buf.at[-(s - 1 + there) * d % NZ, :, units]
        if kind == "yA":
            return self.buf.at[0, -(s - 1 + there) * d % NY, self.units(0, *part_a, d if s == 2 else 0)]
        column = label[1]
        if kind == "yB":
            return self.buf.at[column, -(s - 1 + there) * d % NY, self.units(0, *part_b, d if s == 2 else 0)]
        if kind == "DA":
            return self.buf.at[column, :, self.units(there, *part_a)]
        return self.buf.at[column, slice(None) if d is None else d, self.units(there, *part_b)]

    def copy(self, label):
        i = LABELS[label]
        kind = label[0]
        way = kind[0] if kind[0] == "D" else (kind[0], label[2] if kind == "zA" else label[-1])
        return pltpu.make_async_remote_copy(
            self.place(label, 0), self.place(label, 1), self.send.at[i], self.recv.at[i],
            device_id=self.targets[way], device_id_type=MESH,
        )

    def step(self, k):
        for label in STEPS[k][0]:
            if label not in self.here:
                self.here.add(label)
                self.copy(label).wait_recv()
        for label in STEPS[k][1]:
            cp = self.copy(label)
            cp.start()
            self.started.append(cp)

    def finish(self):
        for cp in self.started:
            cp.wait_send()
        self.started = []


def kernel(
    noise1_hbm, noise2_hbm, root1_hbm, root2_hbm, cond_hbm, cond_ids, krig_hbm, stencil,
    out1, out2, out_map, krig_in,
    weights, noise, roots, fields1, fields2, whole, mine, theirs, field_map, away_whole, away_halved,
    local, krig_send, krig_recv, x_send, x_recv, map_send, map_recv, *by_part,
):
    parts = range(len(PARTS))
    g1, g2, picked, g1_send, g1_recv, g2_send, g2_recv = (
        by_part[len(PARTS) * i : len(PARTS) * (i + 1)] for i in range(7)
    )
    blk, x = lax.axis_index("blk"), lax.axis_index("fld")
    z, y, c = blk // (NY * NC), lax.rem(blk // NC, NY), lax.rem(blk, NC)
    near, far = x + 1 - 2 * lax.rem(x, 2), NX - 1 - x

    def device(dz, dy, dc):
        zz, yy, cc = lax.rem(z + dz + NZ, NZ), lax.rem(y + dy + NY, NY), lax.rem(c + dc, NC)
        return ((zz * NY + yy) * NC + cc, x)

    targets = {("z", d): device(d, 0, 0) for d in (1, -1)}
    targets |= {("y", d): device(0, d, 0) for d in (1, -1)}
    targets["D"] = device(0, 0, 1)
    first = [Gather(g1[p], g1_send[p], g1_recv[p], targets, PARTS[p]) for p in parts]
    second = [Gather(g2[p], g2_send[p], g2_recv[p], targets, PARTS[p]) for p in parts]

    def along(r):
        return (blk, lax.rem(x + r + NX, NX))

    barrier = pltpu.get_barrier_semaphore()
    for to in [*targets.values(), along(1), along(2), along(3)]:
        pl.semaphore_signal(barrier, inc=1, device_id=to, device_id_type=MESH)

    counter = iter(range(100))

    def load(src, dst):
        cp = pltpu.make_async_copy(src, dst, local.at[next(counter)])
        cp.start()
        return cp

    loads = [load(noise1_hbm, noise.at[0]), load(root1_hbm, roots.at[0])]
    for cp in loads:
        cp.wait()

    def sites(b):
        return pl.ds(pl.multiple_of(b * W, W), W)

    def rows_of(p):
        return UNIT * sum(part[0] for part in PARTS[:p]), UNIT * PARTS[p][0]

    def block_of(g, p, i):
        kz, ky = ((i >> 6) - z) & (NZ - 1), ((i >> 4) - y) & (NY - 1)
        per = PARTS[p][0]
        at = pl.ds(((((i >> 3) - c) & 1) * NB + (i & (NB - 1))) * per, per)
        return g[p][kz, ky, at].reshape(per * UNIT, W)

    def put(g, out, p, b, block):
        per = PARTS[p][0]
        lo, n = rows_of(p)
        g[p][0, 0, pl.ds(b * per, per)] = block.reshape(per, UNIT, W)
        out[lo : lo + n, sites(b)] = block

    @pl.loop(0, NB)
    def _(b):
        block = f32dot(noise[0, :, sites(b)], roots[0, b]).astype(jnp.bfloat16)
        for p in parts:
            lo, n = rows_of(p)
            put(g1, fields1, p, b, block[lo : lo + n])

    pl.semaphore_wait(barrier, 8)
    first[0].step(0)

    def krig_copy(i, src, dst, to):
        return pltpu.make_async_remote_copy(
            src, dst, krig_send.at[i], krig_recv.at[i], device_id=to, device_id_type=MESH
        )

    def whole_copy(t, r):
        return krig_copy(3 * t + r - 1, krig_hbm.at[t], krig_in.at[3 * t + r - 1], along(-r))

    def passed_copy(t, d):
        half = pl.ds(0 if d == 1 else K // 2, K // 2)
        src, dst = krig_in.at[3 * t + (2 if d == 1 else 0), half], krig_in.at[3 * t + 1, half]
        return krig_copy(3 * t + 1 if d == 1 else 3 * WHOLE + HALVED + t, src, dst, along(d))

    def halved_copy(t):
        i = 3 * WHOLE + t
        return krig_copy(i, krig_hbm.at[WHOLE + t], krig_in.at[i], (blk, near if t == 0 else far))

    krig_sends = [whole_copy(t, r) for t in range(WHOLE) for r in (3, 1)] + [halved_copy(t) for t in range(HALVED)]
    for cp in krig_sends:
        cp.start()
    noise2_load, root2_load = load(noise2_hbm, noise.at[1]), load(root2_hbm, roots.at[1])
    cond_loads = [load(cond_hbm.at[b], weights.at[b]) for b in range(NB)]
    out_copies = [load(fields1, out1)]

    def pass_weights():
        for t in range(WHOLE):
            for r, d in ((3, 1), (1, -1)):
                whole_copy(t, r).wait_recv()
                cp = passed_copy(t, d)
                cp.start()
                krig_sends.append(cp)

    def second_block(p, b):
        lo, n = rows_of(p)
        for k in range(COND):
            picked[p][:, k * W : (k + 1) * W] = block_of(g1, p, cond_ids[b, k])
        total = f32dot(picked[p][...], weights[b]) + f32dot(noise[1, lo : lo + n, sites(b)], roots[1, b])
        put(g2, fields2, p, b, total.astype(jnp.bfloat16))

    def second_blocks(p, lo, hi):
        return lambda: pl.loop(lo, hi)(lambda b: second_block(p, b))

    def cells(r):
        return pl.ds(CELLS * (r % 2), CELLS)

    whole_loads, halved_loads = [[] for _ in range(WHOLE)], [[] for _ in range(HALVED)]

    def load_whole():
        for t in range(WHOLE):
            whole_loads[t].append(load(krig_hbm.at[t], weights.at[2 * t, :, cells(0)]))
            for r in (1, 3):
                whole_loads[t].append(load(krig_in.at[3 * t + r - 1], weights.at[2 * t + r // 2, :, cells(r)]))

    def load_halved():
        for t in range(HALVED):
            halved_copy(t).wait_recv()
            halved_loads[t].append(load(krig_hbm.at[WHOLE + t], weights.at[2 * WHOLE + t, :, cells(0)]))
            halved_loads[t].append(load(krig_in.at[3 * WHOLE + t], weights.at[2 * WHOLE + t, :, cells(1)]))

    def load_passed():
        for t in range(WHOLE):
            for d in (1, -1):
                passed_copy(t, d).wait_recv()
            whole_loads[t].append(load(krig_in.at[3 * t + 1], weights.at[2 * t + 1, :, cells(2)]))

    def pick(p, t, into):
        lo, n = rows_of(p)
        for s in range(STEN):
            i = stencil[t, s]
            one = block_of(g1, p, jnp.minimum(i, NB1 - 1))
            two = block_of(g2, p, jnp.maximum(i - NB1, 0))
            into[lo : lo + n, s * W : (s + 1) * W] = jnp.where(i < NB1, one, two)

    def field_copy(p, t):
        rows = pl.ds(*rows_of(p))
        i = HALVED * p + t
        return pltpu.make_async_remote_copy(
            mine.at[t, rows], theirs.at[t, rows], x_send.at[i], x_recv.at[i],
            device_id=(blk, far if t == 0 else near), device_id_type=MESH,
        )

    sends = []

    def send(cp):
        cp.start()
        sends.append(cp)

    def exchange(p, t):
        pick(p, WHOLE + t, mine.at[t])
        send(field_copy(p, t))

    def wait_cond():
        for cp in [noise2_load, root2_load] + cond_loads:
            cp.wait()

    def copy_second():
        out_copies.append(load(fields2, out2))

    other = [wait_cond] + [second_blocks(p, b, b + 2) for p in parts for b in range(0, NB, 2)]
    other += [pass_weights, load_whole, copy_second, first[0].finish, first[1].finish]
    other += [functools.partial(exchange, 0, t) for t in range(HALVED)]
    other += [functools.partial(pick, 0, t, whole.at[t]) for t in range(WHOLE)]
    other += [load_halved, second[0].finish]
    for k in ORDER:
        if k < 100:
            other[k]()
        else:
            (first + second)[k // 100 - 1].step(k % 100)

    for t in range(HALVED):
        exchange(1, t)
    load_passed()
    second[1].finish()

    def fields_of(device):
        return pl.ds(pl.multiple_of(device * ROWS, ROWS), ROWS)

    def map_copy(i, src, t, device, to):
        return pltpu.make_async_remote_copy(
            src, field_map.at[t, fields_of(device)], map_send.at[i], map_recv.at[i], device_id=to, device_id_type=MESH
        )

    for t in range(WHOLE):
        pick(1, t, whole.at[t])
        for cp in whole_loads[t]:
            cp.wait()
        for h in range(2):
            total = f32dot(whole[t], weights[2 * t + h])
            for r in (2 * h, 2 * h + 1):
                part = total[:, (r % 2) * CELLS : (r % 2 + 1) * CELLS]
                if r == 0:
                    field_map[t, fields_of(x), :] = part
                else:
                    away_whole[t, r - 1] = part
                    send(map_copy(3 * t + r - 1, away_whole.at[t, r - 1], t, x, along(r)))
    for h in range(2):
        for t in range(HALVED):
            if h == 0:
                for cp in halved_loads[t]:
                    cp.wait()
            else:
                for p in parts:
                    field_copy(p, t).wait_recv()
            total = f32dot((theirs if h else mine)[t], weights[2 * WHOLE + t])
            whose = (far if t == 0 else near) if h else x
            field_map[WHOLE + t, fields_of(whose), :] = total[:, :CELLS]
            away_halved[t, h] = total[:, CELLS:]
            send(map_copy(3 * WHOLE + 2 * t + h, away_halved.at[t, h], WHOLE + t, whose, (blk, near if t == 0 else far)))
    for t in range(WHOLE):
        for r in range(1, NX):
            map_copy(3 * t + r - 1, away_whole.at[t, r - 1], t, lax.rem(x - r + NX, NX), along(r)).wait_recv()
        out_copies.append(load(field_map.at[t], out_map.at[t]))
    for t in range(HALVED):
        for h in range(2):
            mate = near if t == 0 else far
            device = mate if h == 0 else (NX - 1 - mate if t == 0 else mate + 1 - 2 * lax.rem(mate, 2))
            map_copy(3 * WHOLE + 2 * t + h, away_halved.at[t, h], WHOLE + t, device, (blk, mate)).wait_recv()
        out_copies.append(load(field_map.at[WHOLE + t], out_map.at[WHOLE + t]))
    for cp in krig_sends + sends:
        cp.wait_send()
    for cp in out_copies:
        cp.wait()


def hand_out(first_in, second_in, map_in, first_out, second_out, map_out, held, tiles, turned, sem):
    def copy(src, dst, i):
        cp = pltpu.make_async_copy(src, dst, sem.at[i])
        cp.start()
        return cp

    tile_in = copy(map_in, tiles, 0)
    fields_in = [copy(src, held.at[i], 1 + i) for i, src in enumerate((first_in, second_in))]
    out = []
    for i, dst in enumerate((first_out, second_out)):
        if i == 0:
            tile_in.wait()
            for t in range(TILES):
                turned[:, t, :] = tiles[t]
            out.append(copy(turned, map_out, 3))
        fields_in[i].wait()
        out.append(copy(held.at[i], dst, 4 + i))
    for cp in out:
        cp.wait()


def on_device(
    first_noise, second_noise, first_root, second_root, cond_weight, cond_ids, krig_weight, stencil
):
    bf16, f32 = jnp.bfloat16, jnp.float32
    hbm, smem = (pl.BlockSpec(memory_space=m) for m in (pl.ANY, pltpu.SMEM))
    n = len(LABELS)
    dma = pltpu.SemaphoreType.DMA
    fields = jax.ShapeDtypeStruct((ROWS, NB * W), bf16)
    by_part = [pltpu.VMEM((NZ, NY, NC * NB * p[0], UNIT, W), bf16) for p in PARTS] * 2
    by_part += [pltpu.VMEM((p[0] * UNIT, COND * W), bf16) for p in PARTS]
    by_part += [dma((n,))] * (4 * len(PARTS))
    first_fields, second_fields, tiles, _ = pl.pallas_call(
        kernel,
        out_shape=(
            fields,
            fields,
            jax.ShapeDtypeStruct((TILES, NX * ROWS, CELLS), f32),
            jax.ShapeDtypeStruct((3 * WHOLE + HALVED, K, CELLS), bf16),
        ),
        in_specs=[hbm, hbm, hbm, hbm, hbm, smem, hbm, smem],
        out_specs=(hbm, hbm, hbm, hbm),
        scratch_shapes=[
            pltpu.VMEM((NB, COND * W, W), bf16),
            pltpu.VMEM((2, ROWS, NB * W), bf16),
            pltpu.VMEM((2, NB, W, W), bf16),
            pltpu.VMEM((ROWS, NB * W), bf16),
            pltpu.VMEM((ROWS, NB * W), bf16),
            pltpu.VMEM((WHOLE, ROWS, K), bf16),
            pltpu.VMEM((HALVED, ROWS, K), bf16),
            pltpu.VMEM((HALVED, ROWS, K), bf16),
            pltpu.VMEM((TILES, NX * ROWS, CELLS), f32),
            pltpu.VMEM((WHOLE, NX - 1, ROWS, CELLS), f32),
            pltpu.VMEM((HALVED, 2, ROWS, CELLS), f32),
            dma((40,)),
            dma((4 * WHOLE + HALVED,)), dma((4 * WHOLE + HALVED,)),
            dma((HALVED * len(PARTS),)), dma((HALVED * len(PARTS),)),
            dma((3 * WHOLE + 2 * HALVED,)), dma((3 * WHOLE + 2 * HALVED,)),
            *by_part,
        ],
        compiler_params=pltpu.CompilerParams(
            collective_id=0, has_side_effects=True, vmem_limit_bytes=60 << 20
        ),
        cost_estimate=pl.CostEstimate(flops=2300000000, bytes_accessed=30000000, transcendentals=0),
    )(
        first_noise, second_noise, first_root, second_root,
        cond_weight.reshape(NB, COND * W, W), cond_ids,
        krig_weight.reshape(TILES, K, CELLS), stencil,
    )
    field_map = jax.ShapeDtypeStruct((NX * ROWS, TILES, CELLS), f32)
    return pl.pallas_call(
        hand_out,
        out_shape=(fields, fields, field_map),
        in_specs=[hbm, hbm, hbm],
        out_specs=(hbm, hbm, hbm),
        scratch_shapes=[
            pltpu.VMEM((2, ROWS, NB * W), bf16),
            pltpu.VMEM((TILES, NX * ROWS, CELLS), f32),
            pltpu.VMEM((NX * ROWS, TILES, CELLS), f32),
            dma((6,)),
        ],
    )(first_fields, second_fields, tiles)


def solution(mesh):
    placed = (
        P("fld", "blk"),
        P("fld", "blk"),
        P("blk", None, None),
        P("blk", None, None),
        P("blk", None, None, None),
        P("blk", None),
        P("blk", None, None, "fld"),
        P("blk", None),
    )
    return jax.shard_map(
        on_device,
        mesh=mesh,
        in_specs=placed,
        out_specs=(P("fld", "blk"), P("fld", "blk"), P(None, "blk", "fld")),
        check_vma=False,
    )
```
